32 devices in a mesh: gx: 8 (over y, x, core), gy: 4 (over z).
Axes of the slice: x: 2, y: 2, z: 4, core: 2. Of those that a mesh axis runs over, the one named last changes fastest.
Arguments:
- state: float32 [4, 64, 128, 512], P(None, None, 'gx', 'gy'), may hold values from -6 to 6
- damping: float32 [4, 64], replicated, may hold values from 0.02 to 0.2
- k_longwave: float32 [8, 4], replicated, may hold values from 0.02 to 0.2
- k_shortwave: float32 [8, 4], replicated, may hold values from 0.02 to 0.2
- solar: float32 [8], replicated, may hold values from 2 to 8
- daylight: int32 [4, 128], P('gy'), may hold values from 0 to 1, as said below
- cloud_top: int32 [4, 128], P('gy'), may hold values from 0 to 64
Outputs:
- updated: float32 [4, 64, 128, 512], P(None, None, 'gx', 'gy')
The draws below stay inside these ranges and needn't reach their ends.
Inputs may be any that keep to these rules, and one draw needn't show every extreme that they name: daylight is the same on the 16 rows of one gx index; in each column tile, the gx indices g and g + 8 / 2 (modulo 8) have opposite daylight.
All inputs are finite; a program needn't handle non-finite values.
Results may differ from the reference program's by a relative error of at most 0.0003.
Values sent between devices are 32-bit elements; how exact they have to be, the bound alone decides.
A program may use at most 128 MiB of HBM per device.

```python
import math
import jax
import jax.numpy as jnp
from jax import lax

FIELDS = 4
LEV = 64
LWB = 8
SWB = 8
COLS = 128
R_DEV = 16
NR = 128
NC = 512
N_GX = 8
N_GY = 4


def draw_daylight(key, part):
    base_key = jax.random.fold_in(key, 7)
    cycle_size = NR // R_DEV
    half_cycle = cycle_size // 2

    def per_column(column_key):
        sun_phase = jax.random.randint(column_key, (), 0, cycle_size)
        shifted = (jnp.arange(cycle_size, dtype=jnp.int32) - sun_phase) % cycle_size
        is_day = shifted < half_cycle
        day_flags = jnp.broadcast_to(is_day[:, None], (cycle_size, R_DEV)).astype(jnp.int32)
        return day_flags.reshape(-1)
    column_keys = jax.random.split(base_key, NC // COLS)
    return jax.vmap(per_column)(column_keys)


def set_ends(values, own_key, least, largest):
    longest = values.shape.index(max(values.shape))
    spots = []
    for shift in (0, 1):
        where = [jax.random.randint(jax.random.fold_in(own_key, axis), (), 0, length) for axis, length in enumerate(values.shape)]
        where[longest] = (where[longest] + shift) % values.shape[longest]
        spots.append(tuple(where))
    return values.at[spots[0]].set(least).at[spots[1]].set(largest)


def level_of(own_key, dims, shards, least, high):
    def one(position, parts):
        steps = jax.random.uniform(jax.random.fold_in(jax.random.fold_in(own_key, 6), position), (parts,), jnp.float32, least / len(shards), high / len(shards))
        return jnp.repeat(jnp.exp(steps), dims[position] // parts).reshape((-1,) + (1,) * (len(dims) - position - 1))

    loudness = one(*shards[0])
    for cut in shards[1:]:
        loudness = loudness * one(*cut)
    return loudness


def bell_draw(rng, extent, spread, reach, shards=(), kind=jnp.bfloat16):
    factor_of = level_of(rng, extent, shards, -0.22, 0.18) if shards else 1.0
    drawn = jax.random.normal(rng, extent, jnp.float32) * spread * factor_of
    return jnp.minimum(jnp.maximum(drawn, -reach), reach).astype(kind)


def setup_inputs(seed: int = 0) -> dict:
    key_list = jax.random.split(jax.random.key(seed), 8)
    return {
        "state": bell_draw(key_list[0], (FIELDS, LEV, NR, NC), 1.0, 6.0, ((2, 8), (3, 4)), jnp.float32),
        "damping": jnp.clip(jnp.exp(jax.random.uniform(key_list[1], (FIELDS, LEV), jnp.float32, math.log(0.02), math.log(0.2))), 0.02, 0.2),
        "k_longwave": jnp.clip(jnp.exp(jax.random.uniform(key_list[2], (LWB, FIELDS), jnp.float32, math.log(0.02), math.log(0.2))), 0.02, 0.2),
        "k_shortwave": jnp.clip(jnp.exp(jax.random.uniform(key_list[3], (SWB, FIELDS), jnp.float32, math.log(0.02), math.log(0.2))), 0.02, 0.2),
        "solar": jnp.clip(jnp.exp(jax.random.uniform(key_list[4], (SWB,), jnp.float32, math.log(2.0), math.log(8.0))), 2.0, 8.0),
        "daylight": draw_daylight(jax.random.fold_in(key_list[7], 71), 0),
        "cloud_top": set_ends(jax.random.randint(key_list[6], (N_GY, NR), 0, LEV + 1), jax.random.fold_in(key_list[6], 1), 0, LEV).astype(jnp.int32),
    }


time_step = 0.1


def solve_levels(optical, source):
    coupling = jnp.concatenate([20.0 * jnp.exp(-0.1 * optical[:-1]), jnp.zeros_like(optical[:1])], 0)
    coupling_below = jnp.concatenate([jnp.zeros_like(optical[:1]), coupling[:-1]], 0)
    diagonal = 1.0 + optical + coupling_below + coupling

    def forward(state_pair, inputs):
        factor_prev, value_prev = state_pair
        diag_here, below_here, above_here, source_here = inputs
        pivot_value = diag_here - below_here * factor_prev
        factor = above_here / pivot_value
        value = (source_here + below_here * value_prev) / pivot_value
        return (factor, value), (factor, value)

    zeros_row = jnp.zeros_like(optical[0])
    _, (factors, values) = lax.scan(forward, (zeros_row, zeros_row), (diagonal, coupling_below, coupling, source), unroll=16)

    def backward(next_value, inputs):
        factor, value = inputs
        result = value + factor * next_value
        return result, result

    _, radiance = lax.scan(backward, zeros_row, (factors, values), reverse=True, unroll=16)
    return radiance


def band_depth(absorb, amount, cloudy, cloud_depth):
    summed = absorb[None, :, 0, None, None] * amount[:, None, 0]
    for field in range(1, amount.shape[1]):
        summed = summed + absorb[None, :, field, None, None] * amount[:, None, field]
    return summed + cloud_depth * cloudy[:, None]


def physics(fields, cloud_tops, daylit, sw_rows, sw_slot, k_longwave, k_shortwave, solar):
    levels = jnp.arange(fields.shape[2], dtype=jnp.int32)
    cloudy = (levels[None, :] >= cloud_tops[:, None]).astype(jnp.float32)[:, :, None]
    amount = fields * fields
    emission = jnp.exp(0.3 * jnp.tanh(fields[:, 0]))
    depth_lw = band_depth(k_longwave, amount, cloudy, 0.5)
    radiance_lw = solve_levels(jnp.moveaxis(depth_lw, 2, 0), jnp.moveaxis(depth_lw * emission[:, None], 2, 0))
    radiance_lw = jnp.moveaxis(radiance_lw, 0, 2)
    lw_heat = jnp.sum(depth_lw * (radiance_lw - emission[:, None]), 1)
    sub_amount = jnp.take(amount, sw_rows, axis=0)
    sub_cloudy = jnp.take(cloudy, sw_rows, axis=0)
    depth_sw = band_depth(k_shortwave, sub_amount, sub_cloudy, 0.3)
    sw_source = solar[None, :, None, None] * (1.0 - jnp.exp(-depth_sw))
    radiance_sw = jnp.moveaxis(solve_levels(jnp.moveaxis(depth_sw, 2, 0), jnp.moveaxis(sw_source, 2, 0)), 0, 2)
    sw_part = jnp.sum(depth_sw * radiance_sw, 1)
    sw_heat = jnp.where(daylit[:, None, None] == 1, jnp.take(sw_part, sw_slot, axis=0), 0.0)
    moist = -2.0 * cloudy * fields[:, 1]
    return jnp.stack([lw_heat + sw_heat, moist], 1)


def reference(state, damping, k_longwave, k_shortwave, solar, daylight, cloud_top):
    laplace = jnp.roll(state, 1, 2) + jnp.roll(state, -1, 2) + jnp.roll(state, 1, 3) + jnp.roll(state, -1, 3) - 4.0 * state
    damped = state + damping[:, :, None, None] * laplace
    tile_list = []
    for column in range(N_GY):
        tile_part = damped[:, :, :, column * COLS:(column + 1) * COLS]
        group_blocks = jnp.transpose(tile_part, (2, 0, 1, 3)).reshape(N_GX, R_DEV, FIELDS, LEV, COLS)
        group_tops = cloud_top[column].reshape(N_GX, R_DEV)
        group_days = daylight[column].reshape(N_GX, R_DEV)

        def per_group(group_args):
            blocks_here, tops_here, days_here = group_args
            row_iota = jnp.arange(R_DEV, dtype=jnp.int32)
            tendency = physics(blocks_here, tops_here, days_here, row_iota, row_iota, k_longwave, k_shortwave, solar)
            return blocks_here.at[:, :2].add(time_step * tendency)

        renewed = lax.map(per_group, (group_blocks, group_tops, group_days))
        tile_list.append(jnp.transpose(renewed.reshape(NR, FIELDS, LEV, COLS), (1, 2, 0, 3)))
    return jnp.concatenate(tile_list, 3)
```

```python
import math

import jax
import numpy as np
import jax.numpy as jnp
from jax import lax
from jax.experimental import pallas as pl
from jax.experimental.pallas import tpu as pltpu
from jax.sharding import PartitionSpec as P

time_step = 0.1
F32 = jnp.float32
BF16 = jnp.bfloat16
LOG2E = math.log2(math.e)
PARTS = 14


def split(value):
    high = value.astype(BF16)
    low = (value - high.astype(F32)).astype(BF16)
    return high, low


def build_mixing(mix, k_ref, first, cloud_depth, rows):
    bands = k_ref.shape[0]
    width = mix.shape[1]
    group = lax.broadcasted_iota(jnp.int32, (bands, width), 1) // rows
    k_high, k_low = split(k_ref[...])
    k_high, k_low = k_high.astype(F32), k_low.astype(F32)
    cloud_high = float(np.asarray(cloud_depth, dtype=BF16))
    spread = jnp.where(group == 12, cloud_high, jnp.where(group == 13, cloud_depth - cloud_high, 0.0))
    for field in range(4):
        high = jnp.broadcast_to(k_high[:, field : field + 1], (bands, width))
        low = jnp.broadcast_to(k_low[:, field : field + 1], (bands, width))
        spread = jnp.where((group == field) | (group == field + 8), high, spread)
        spread = jnp.where(group == field + 4, low, spread)
    lane = lax.broadcasted_iota(jnp.int32, (rows, width), 1)
    row = lax.broadcasted_iota(jnp.int32, (rows, width), 0)
    own = lane % rows == row
    for band in range(bands):
        block = jnp.broadcast_to(spread[band : band + 1], (rows, width))
        mix[(first + band) * rows : (first + band + 1) * rows] = jnp.where(own, block, 0.0).astype(BF16)


def kernel(
    damping, solar, state, north, south, sides, k_lw, k_sw, daylight, cloud_top, out,
    mix, emit, depth, factors, values,
):
    fields, levels, rows, cols = state.shape
    lwb, swb = k_lw.shape[0], k_sw.shape[0]
    bands = lwb + swb
    half = 8
    me = lax.axis_index("gx")

    build_mixing(mix, k_lw, 0, 0.5, rows)
    build_mixing(mix, k_sw, lwb, 0.3, rows)

    lane = lax.broadcasted_iota(jnp.int32, (rows, cols), 1)
    row = lax.broadcasted_iota(jnp.int32, (rows, cols), 0)
    total = cloud_top.shape[1]
    wide_lane = lax.broadcasted_iota(jnp.int32, (rows, total), 1)
    wide_row = lax.broadcasted_iota(jnp.int32, (rows, total), 0)
    mine = wide_lane == me * rows + wide_row
    tops = jnp.sum(jnp.where(mine, cloud_top[...].astype(F32), 0.0), axis=1, keepdims=True)
    tops = jnp.broadcast_to(tops, (rows, cols)).astype(jnp.int32)
    days = jnp.sum(jnp.where(mine, daylight[...].astype(F32), 0.0), axis=1, keepdims=True)
    days = time_step * jnp.broadcast_to(days, (rows, cols))

    def damp_level(level):
        cloudy = jnp.where(level >= tops, 1.0, 0.0).astype(F32)
        highs, lows = [], []
        for field in range(fields):
            centre = state[field, level]
            up = jnp.where(row == 0, north[field, pl.ds(level, 1)], pltpu.roll(centre, 1, 0))
            down = jnp.where(row == rows - 1, south[field, pl.ds(level, 1)], pltpu.roll(centre, rows - 1, 0))
            side = pltpu.roll(sides[field], lax.rem(cols - 2 * level, cols), 1)
            left = jnp.where(lane == 0, side, pltpu.roll(centre, 1, 1))
            right = jnp.where(lane == cols - 1, side, pltpu.roll(centre, cols - 1, 1))
            laplace = (up + down) + (left + right) - 4.0 * centre
            damped = centre + damping[field, level] * laplace
            if field == 0:
                emit[level] = jnp.exp(0.3 * jnp.tanh(damped))
            if field == 1:
                out[field, level] = damped - (2.0 * time_step) * cloudy * damped
            else:
                out[field, level] = damped
            high, low = split(damped * damped)
            highs.append(high)
            lows.append(low)
        cloud = cloudy.astype(BF16)
        return jnp.concatenate(highs + highs + lows + [cloud, cloud], 0)

    @pl.loop(0, levels // 2)
    def _(pair):
        operand = jnp.concatenate([damp_level(2 * pair), damp_level(2 * pair + 1)], 1)
        result = jnp.dot(mix[...], operand, preferred_element_type=F32)
        depth[2 * pair] = result[:, :cols]
        depth[2 * pair + 1] = result[:, cols:]

    zero = jnp.zeros((half, cols), F32)
    log20 = math.log2(20.0)

    for part in range(rows // half):
        at = [band * rows + part * half for band in range(bands)]
        here = slice(part * half, (part + 1) * half)

        def forward(level, carry):
            carry = list(carry)
            emission = emit[level, here]
            last = jnp.where(level == levels - 1, 0.0, 1.0).astype(F32)
            for band in range(bands):
                g, h = carry[2 * band], carry[2 * band + 1]
                d = depth[level, at[band] : at[band] + half]
                coupling = last * jnp.exp2(log20 - (0.1 * LOG2E) * d)
                if band < lwb:
                    source = d * emission
                else:
                    source = solar[band - lwb] * (1.0 - jnp.exp2(-LOG2E * d))
                q = (1.0 + d) + g
                w = source + h
                r = pl.reciprocal(q + coupling, approx=True)
                factor = coupling * r
                factors[level, at[band] : at[band] + half] = factor
                values[level, at[band] : at[band] + half] = w * r
                carry[2 * band], carry[2 * band + 1] = factor * q, factor * w
            return tuple(carry)

        lax.fori_loop(0, levels, forward, (zero,) * (2 * bands))

        def backward(step, carry):
            carry = list(carry)
            level = levels - 1 - step
            emission = emit[level, here]
            lw, sw = zero, zero
            for band in range(bands):
                d = depth[level, at[band] : at[band] + half]
                x = (
                    values[level, at[band] : at[band] + half]
                    + factors[level, at[band] : at[band] + half] * carry[band]
                )
                carry[band] = x
                if band < lwb:
                    lw = lw + d * (x - emission)
                else:
                    sw = sw + d * x
            out[0, level, here] = out[0, level, here] + (time_step * lw + days[here] * sw)
            return tuple(carry)

        lax.fori_loop(0, levels, backward, (zero,) * bands)


def shards(state, damping, k_longwave, k_shortwave, solar, daylight, cloud_top):
    fields, levels, rows, cols = state.shape
    bands = k_longwave.shape[0] + k_shortwave.shape[0]

    def ring(axis, step):
        count = lax.axis_size(axis)
        return [(i, (i + step) % count) for i in range(count)]

    north = lax.ppermute(state[:, :, rows - 1], "gx", ring("gx", 1))
    south = lax.ppermute(state[:, :, 0], "gx", ring("gx", -1))
    west = lax.ppermute(jnp.swapaxes(state[:, :, :, cols - 1], 1, 2), "gy", ring("gy", 1))
    east = lax.ppermute(jnp.swapaxes(state[:, :, :, 0], 1, 2), "gy", ring("gy", -1))
    sides = jnp.stack([west, jnp.roll(east, -1, 2)], 3).reshape(fields, rows, 2 * levels)
    vmem = pl.BlockSpec(memory_space=pltpu.VMEM)
    smem = pl.BlockSpec(memory_space=pltpu.SMEM)
    return pl.pallas_call(
        kernel,
        out_shape=jax.ShapeDtypeStruct(state.shape, F32),
        in_specs=[smem, smem] + [vmem] * 8,
        out_specs=vmem,
        scratch_shapes=[
            pltpu.VMEM((bands * rows, PARTS * rows), BF16),
            pltpu.VMEM((levels, rows, cols), F32),
            pltpu.VMEM((levels, bands * rows, cols), F32),
            pltpu.VMEM((levels, bands * rows, cols), F32),
            pltpu.VMEM((levels, bands * rows, cols), F32),
        ],
        compiler_params=pltpu.CompilerParams(vmem_limit_bytes=48 * 1024 * 1024),
        cost_estimate=pl.CostEstimate(flops=100_000_000, bytes_accessed=4_000_000, transcendentals=5_000_000),
    )(damping, solar, state, north, south, sides, k_longwave, k_shortwave, daylight, cloud_top)


def solution(mesh):
    in_specs = (P(None, None, "gx", "gy"), P(), P(), P(), P(), P("gy", None), P("gy", None))
    out_specs = P(None, None, "gx", "gy")
    return jax.shard_map(shards, mesh=mesh, in_specs=in_specs, out_specs=out_specs, check_vma=False)
```

```python
import functools
import math

import jax
import numpy as np
import jax.numpy as jnp
from jax import lax
from jax.experimental import pallas as pl
from jax.experimental.pallas import tpu as pltpu
from jax.sharding import PartitionSpec as P

time_step = 0.1
F32 = jnp.float32
BF16 = jnp.bfloat16
LOG2E = math.log2(math.e)
PARTS = 14


PAIRS, AHEAD, BACK = 2, 4, 4


def split(value):
    high = value.astype(BF16)
    low = (value - high.astype(F32)).astype(BF16)
    return high, low


def build_mixing(mix, k_ref, first, cloud_depth, rows):
    bands = k_ref.shape[0]
    width = mix.shape[1]
    group = lax.broadcasted_iota(jnp.int32, (bands, width), 1) // rows
    k_high, k_low = split(k_ref[...])
    k_high, k_low = k_high.astype(F32), k_low.astype(F32)
    cloud_high = float(np.asarray(cloud_depth, dtype=BF16))
    spread = jnp.where(group == 12, cloud_high, jnp.where(group == 13, cloud_depth - cloud_high, 0.0))
    for field in range(4):
        high = jnp.broadcast_to(k_high[:, field : field + 1], (bands, width))
        low = jnp.broadcast_to(k_low[:, field : field + 1], (bands, width))
        spread = jnp.where((group == field) | (group == field + 8), high, spread)
        spread = jnp.where(group == field + 4, low, spread)
    lane = lax.broadcasted_iota(jnp.int32, (rows, width), 1)
    row = lax.broadcasted_iota(jnp.int32, (rows, width), 0)
    own = lane % rows == row
    for band in range(bands):
        block = jnp.broadcast_to(spread[band : band + 1], (rows, width))
        mix[(first + band) * rows : (first + band + 1) * rows] = jnp.where(own, block, 0.0).astype(BF16)


def exchange(shape, state, north, south, west, east, first, final, packed, send, recv):
    n_gx, n_gy = shape
    fields, levels, rows, cols = state.shape
    gx, gy = lax.axis_index("gx"), lax.axis_index("gy")
    after, before = lax.rem(gx + 1, n_gx), lax.rem(gx + n_gx - 1, n_gx)
    right, left = lax.rem(gy + 1, n_gy), lax.rem(gy + n_gy - 1, n_gy)
    peers = ({"gx": after}, {"gx": before}, {"gy": right}, {"gy": left})

    barrier = pltpu.get_barrier_semaphore()
    for peer in peers:
        pl.semaphore_signal(barrier, inc=1, device_id=peer, device_id_type=pl.DeviceIdType.MESH)
    for field in range(fields):
        first[field] = state[field, :, 0, :]
        final[field] = state[field, :, rows - 1, :]
    pl.semaphore_wait(barrier, 4)

    moves = ((final, north), (first, south), (packed, west), (packed, east))
    copies = [
        pltpu.make_async_remote_copy(
            src_ref=source,
            dst_ref=target,
            send_sem=send.at[index],
            recv_sem=recv.at[index],
            device_id=peers[index],
            device_id_type=pl.DeviceIdType.MESH,
        )
        for index, (source, target) in enumerate(moves)
    ]
    copies[0].start()
    copies[1].start()
    pair = lax.broadcasted_iota(jnp.int32, (rows, cols), 1) // 2

    def pack(step, held):
        held = list(held)
        for inner in range(8):
            level = 8 * step + inner
            for field in range(fields):
                turned = pltpu.roll(state[field, level], 2 * level + 1, 1)
                held[field] = jnp.where(pair == level, turned, held[field])
        return tuple(held)

    held = lax.fori_loop(0, levels // 8, pack, (jnp.zeros((rows, cols), F32),) * fields)
    for field in range(fields):
        packed[field] = held[field]
    copies[2].start()
    copies[3].start()
    for copy in copies:
        copy.wait()


def kernel(
    damping, solar, state, north, south, west, east, k_lw, k_sw, daylight, cloud_top, out,
    mix, sides, emit, depth, factors, values,
):
    fields, levels, rows, cols = state.shape
    lwb, swb = k_lw.shape[0], k_sw.shape[0]
    bands = lwb + swb
    half = 8
    me = lax.axis_index("gx")

    build_mixing(mix, k_lw, 0, 0.5, rows)
    build_mixing(mix, k_sw, lwb, 0.3, rows)

    lane = lax.broadcasted_iota(jnp.int32, (rows, cols), 1)
    row = lax.broadcasted_iota(jnp.int32, (rows, cols), 0)
    total = cloud_top.shape[1]
    wide_lane = lax.broadcasted_iota(jnp.int32, (rows, total), 1)
    wide_row = lax.broadcasted_iota(jnp.int32, (rows, total), 0)
    mine = wide_lane == me * rows + wide_row
    tops = jnp.sum(jnp.where(mine, cloud_top[...].astype(F32), 0.0), axis=1, keepdims=True)
    tops = jnp.broadcast_to(tops, (rows, cols)).astype(jnp.int32)
    days = jnp.sum(jnp.where(mine, daylight[...].astype(F32), 0.0), axis=1, keepdims=True)
    days = time_step * jnp.broadcast_to(days, (rows, cols))

    for field in range(fields):
        turned = pltpu.roll(east[field], cols - 2, 1)
        sides[field] = jnp.where(lane % 2 == 0, west[field], turned)

    def damp_level(level):
        cloudy = jnp.where(level >= tops, 1.0, 0.0).astype(F32)
        highs, lows = [], []
        for field in range(fields):
            centre = state[field, level]
            up = jnp.where(row == 0, north[field, pl.ds(level, 1)], pltpu.roll(centre, 1, 0))
            down = jnp.where(row == rows - 1, south[field, pl.ds(level, 1)], pltpu.roll(centre, rows - 1, 0))
            side = pltpu.roll(sides[field], lax.rem(cols - 2 * level, cols), 1)
            left = jnp.where(lane == 0, side, pltpu.roll(centre, 1, 1))
            right = jnp.where(lane == cols - 1, side, pltpu.roll(centre, cols - 1, 1))
            laplace = (up + down) + (left + right) - 4.0 * centre
            damped = centre + damping[field, level] * laplace
            if field == 0:
                emit[level] = jnp.exp(0.3 * jnp.tanh(damped))
            if field == 1:
                out[field, level] = damped - (2.0 * time_step) * cloudy * damped
            else:
                out[field, level] = damped
            high, low = split(damped * damped)
            highs.append(high)
            lows.append(low)
        cloud = cloudy.astype(BF16)
        return jnp.concatenate(highs + highs + lows + [cloud, cloud], 0)

    @pl.loop(0, levels // (2 * PAIRS))
    def _(step):
        for inner in range(PAIRS):
            level = 2 * (PAIRS * step + inner)
            operand = jnp.concatenate([damp_level(level), damp_level(level + 1)], 1)
            result = jnp.dot(mix[...], operand, preferred_element_type=F32)
            depth[level] = result[:, :cols]
            depth[level + 1] = result[:, cols:]

    zero = jnp.zeros((half, cols), F32)
    log20 = math.log2(20.0)

    for part in range(rows // half):
        at = [band * rows + part * half for band in range(bands)]
        here = slice(part * half, (part + 1) * half)

        def forward(level, carry, last=False):
            carry = list(carry)
            emission = emit[level, here]
            for band in range(bands):
                g, h = carry[2 * band], carry[2 * band + 1]
                d = depth[level, at[band] : at[band] + half]
                if band < lwb:
                    source = d * emission
                else:
                    source = solar[band - lwb] * (1.0 - jnp.exp2(-LOG2E * d))
                q = (1.0 + d) + g
                w = source + h
                if last:
                    factor = zero
                    r = pl.reciprocal(q, approx=True)
                else:
                    coupling = jnp.exp2(log20 - (0.1 * LOG2E) * d)
                    r = pl.reciprocal(q + coupling, approx=True)
                    factor = coupling * r
                    carry[2 * band], carry[2 * band + 1] = factor * q, factor * w
                factors[level, at[band] : at[band] + half] = factor
                values[level, at[band] : at[band] + half] = w * r
            return tuple(carry)

        def forward_steps(step, carry):
            for inner in range(AHEAD):
                carry = forward(AHEAD * step + inner, carry)
            return carry

        carry = lax.fori_loop(0, levels // AHEAD - 1, forward_steps, (zero,) * (2 * bands))
        for level in range(levels - AHEAD, levels):
            carry = forward(level, carry, level == levels - 1)

        def backward(level, carry):
            carry = list(carry)
            emission = emit[level, here]
            lw, sw = zero, zero
            for band in range(bands):
                d = depth[level, at[band] : at[band] + half]
                x = (
                    values[level, at[band] : at[band] + half]
                    + factors[level, at[band] : at[band] + half] * carry[band]
                )
                carry[band] = x
                if band < lwb:
                    lw = lw + d * (x - emission)
                else:
                    sw = sw + d * x
            out[0, level, here] = out[0, level, here] + (time_step * lw + days[here] * sw)
            return tuple(carry)

        def backward_steps(step, carry):
            for inner in range(BACK):
                carry = backward(levels - 1 - BACK * step - inner, carry)
            return carry

        lax.fori_loop(0, levels // BACK, backward_steps, (zero,) * bands)


def shards(state, damping, k_longwave, k_shortwave, solar, daylight, cloud_top):
    fields, levels, rows, cols = state.shape
    bands = k_longwave.shape[0] + k_shortwave.shape[0]

    vmem = pl.BlockSpec(memory_space=pltpu.VMEM)
    smem = pl.BlockSpec(memory_space=pltpu.SMEM)
    edge_rows = jax.ShapeDtypeStruct((fields, levels, cols), F32)
    edge_cols = jax.ShapeDtypeStruct((fields, rows, cols), F32)
    halos = pl.pallas_call(
        functools.partial(exchange, (lax.axis_size("gx"), lax.axis_size("gy"))),
        out_shape=[edge_rows, edge_rows, edge_cols, edge_cols],
        in_specs=[vmem],
        out_specs=[vmem] * 4,
        scratch_shapes=[
            pltpu.VMEM(edge_rows.shape, F32),
            pltpu.VMEM(edge_rows.shape, F32),
            pltpu.VMEM(edge_cols.shape, F32),
            pltpu.SemaphoreType.DMA((4,)),
            pltpu.SemaphoreType.DMA((4,)),
        ],
        compiler_params=pltpu.CompilerParams(
            collective_id=0, has_side_effects=True, vmem_limit_bytes=8 * 1024 * 1024
        ),
        name="exchange",
    )(state)
    return pl.pallas_call(
        kernel,
        out_shape=jax.ShapeDtypeStruct(state.shape, F32),
        in_specs=[smem, smem] + [vmem] * 9,
        out_specs=vmem,
        scratch_shapes=[
            pltpu.VMEM((bands * rows, PARTS * rows), BF16),
            pltpu.VMEM((fields, rows, cols), F32),
            pltpu.VMEM((levels, rows, cols), F32),
            pltpu.VMEM((levels, bands * rows, cols), F32),
            pltpu.VMEM((levels, bands * rows, cols), F32),
            pltpu.VMEM((levels, bands * rows, cols), F32),
        ],
        compiler_params=pltpu.CompilerParams(vmem_limit_bytes=48 * 1024 * 1024),
        cost_estimate=pl.CostEstimate(flops=100_000_000, bytes_accessed=4_000_000, transcendentals=5_000_000),
    )(damping, solar, state, *halos, k_longwave, k_shortwave, daylight, cloud_top)


def solution(mesh):
    in_specs = (P(None, None, "gx", "gy"), P(), P(), P(), P(), P("gy", None), P("gy", None))
    out_specs = P(None, None, "gx", "gy")
    return jax.shard_map(shards, mesh=mesh, in_specs=in_specs, out_specs=out_specs, check_vma=False)
```

```python
import functools
import math

import jax
import numpy as np
import jax.numpy as jnp
from jax import lax
from jax.experimental import pallas as pl
from jax.experimental.pallas import tpu as pltpu
from jax.sharding import PartitionSpec as P

time_step = 0.1
F32 = jnp.float32
BF16 = jnp.bfloat16
LOG2E = math.log2(math.e)
PARTS = 14


PAIRS, AHEAD, BACK = 8, 8, 8


def split(value):
    high = value.astype(BF16)
    low = (value - high.astype(F32)).astype(BF16)
    return high, low


def build_mixing(mix, k_ref, first, cloud_depth, rows):
    bands = k_ref.shape[1]
    width = mix.shape[1]
    group = lax.broadcasted_iota(jnp.int32, (bands, width), 1) // rows
    same = lax.broadcasted_iota(jnp.int32, (bands, bands), 0) == lax.broadcasted_iota(
        jnp.int32, (bands, bands), 1
    )
    cloud_high = float(np.asarray(cloud_depth, dtype=BF16))
    spread = jnp.where(group == 12, cloud_high, jnp.where(group == 13, cloud_depth - cloud_high, 0.0))
    for field in range(4):
        weights = jnp.broadcast_to(k_ref[field : field + 1, :], (bands, bands))
        weights = jnp.sum(jnp.where(same, weights, 0.0), axis=1, keepdims=True)
        high, low = split(jnp.broadcast_to(weights, (bands, width)))
        high, low = high.astype(F32), low.astype(F32)
        spread = jnp.where((group == field) | (group == field + 8), high, spread)
        spread = jnp.where(group == field + 4, low, spread)
    lane = lax.broadcasted_iota(jnp.int32, (rows, width), 1)
    row = lax.broadcasted_iota(jnp.int32, (rows, width), 0)
    own = lane % rows == row
    for band in range(bands):
        block = jnp.broadcast_to(spread[band : band + 1], (rows, width))
        mix[(first + band) * rows : (first + band + 1) * rows] = jnp.where(own, block, 0.0).astype(BF16)


def exchange(
    shape, damping, source, k_lw, k_sw, north, south, west, east, partial, mix,
    state, first, final, packed, load, send, recv,
):
    n_gx, n_gy = shape
    fields, levels, rows, cols = source.shape
    loads = [pltpu.make_async_copy(source.at[field], state.at[field], load.at[field]) for field in range(fields)]
    for copy in loads:
        copy.start()
    gx, gy = lax.axis_index("gx"), lax.axis_index("gy")
    after, before = lax.rem(gx + 1, n_gx), lax.rem(gx + n_gx - 1, n_gx)
    right, left = lax.rem(gy + 1, n_gy), lax.rem(gy + n_gy - 1, n_gy)
    peers = ({"gx": after}, {"gx": before}, {"gy": right}, {"gy": left})

    barrier = pltpu.get_barrier_semaphore()
    for peer in peers:
        pl.semaphore_signal(barrier, inc=1, device_id=peer, device_id_type=pl.DeviceIdType.MESH)
    for field in range(fields):
        loads[field].wait()
        first[field] = state[field, :, 0, :]
        final[field] = state[field, :, rows - 1, :]
    pl.semaphore_wait(barrier, 4)

    moves = ((final, north), (first, south), (packed, west), (packed, east))
    copies = [
        pltpu.make_async_remote_copy(
            src_ref=origin,
            dst_ref=target,
            send_sem=send.at[index],
            recv_sem=recv.at[index],
            device_id=peers[index],
            device_id_type=pl.DeviceIdType.MESH,
        )
        for index, (origin, target) in enumerate(moves)
    ]
    copies[0].start()
    copies[1].start()
    pair = lax.broadcasted_iota(jnp.int32, (rows, cols), 1) // 2

    def pack(step, held):
        held = list(held)
        for inner in range(8):
            level = 8 * step + inner
            for field in range(fields):
                turned = pltpu.roll(state[field, level], 2 * level + 1, 1)
                held[field] = jnp.where(pair == level, turned, held[field])
        return tuple(held)

    held = lax.fori_loop(0, levels // 8, pack, (jnp.zeros((rows, cols), F32),) * fields)
    for field in range(fields):
        packed[field] = held[field]
    copies[2].start()
    copies[3].start()

    build_mixing(mix, k_lw, 0, 0.5, rows)
    build_mixing(mix, k_sw, k_lw.shape[1], 0.3, rows)
    lane = lax.broadcasted_iota(jnp.int32, (rows, cols), 1)
    row = lax.broadcasted_iota(jnp.int32, (rows, cols), 0)

    @pl.loop(0, levels // 4)
    def _(step):
        for inner in range(4):
            level = 4 * step + inner
            for field in range(fields):
                centre = state[field, level]
                up = jnp.where(row == 0, 0.0, pltpu.roll(centre, 1, 0))
                down = jnp.where(row == rows - 1, 0.0, pltpu.roll(centre, rows - 1, 0))
                before_lane = jnp.where(lane == 0, 0.0, pltpu.roll(centre, 1, 1))
                after_lane = jnp.where(lane == cols - 1, 0.0, pltpu.roll(centre, cols - 1, 1))
                laplace = (up + down) + (before_lane + after_lane) - 4.0 * centre
                partial[field, level] = centre + damping[field, level] * laplace

    for copy in copies:
        copy.wait()


def kernel(
    damping, solar, north, south, west, east, partial, mix, daylight, cloud_top, final,
    out, sides, emit, depth, factors, values, finished,
):
    fields, levels, rows, cols = partial.shape
    swb = solar.shape[0]
    bands = mix.shape[0] // rows
    lwb = bands - swb
    half = 8
    me = lax.axis_index("gx")

    lane = lax.broadcasted_iota(jnp.int32, (rows, cols), 1)
    row = lax.broadcasted_iota(jnp.int32, (rows, cols), 0)
    total = cloud_top.shape[1]
    wide_lane = lax.broadcasted_iota(jnp.int32, (rows, total), 1)
    wide_row = lax.broadcasted_iota(jnp.int32, (rows, total), 0)
    mine = wide_lane == me * rows + wide_row
    tops = jnp.sum(jnp.where(mine, cloud_top[...].astype(F32), 0.0), axis=1, keepdims=True)
    tops = jnp.broadcast_to(tops, (rows, cols)).astype(jnp.int32)
    days = jnp.sum(jnp.where(mine, daylight[...].astype(F32), 0.0), axis=1, keepdims=True)
    days = time_step * jnp.broadcast_to(days, (rows, cols))

    for field in range(fields):
        turned = pltpu.roll(east[field], cols - 2, 1)
        sides[field] = jnp.where(lane % 2 == 0, west[field], turned)

    border = (lane == 0) | (lane == cols - 1)

    def damp_level(level):
        cloudy = jnp.where(level >= tops, 1.0, 0.0).astype(F32)
        highs, lows = [], []
        for field in range(fields):
            beside = jnp.where(row == rows - 1, south[field, pl.ds(level, 1)], 0.0)
            beside = jnp.where(row == 0, north[field, pl.ds(level, 1)], beside)
            side = pltpu.roll(sides[field], lax.rem(cols - 2 * level, cols), 1)
            beside = beside + jnp.where(border, side, 0.0)
            damped = partial[field, level] + damping[field, level] * beside
            if field == 0:
                emit[level] = jnp.exp(0.3 * jnp.tanh(damped))
            if field == 1:
                out[field, level] = damped - (2.0 * time_step) * cloudy * damped
            else:
                out[field, level] = damped
            high, low = split(damped * damped)
            highs.append(high)
            lows.append(low)
        cloud = cloudy.astype(BF16)
        return jnp.concatenate(highs + highs + lows + [cloud, cloud], 0)

    @pl.loop(0, levels // (2 * PAIRS))
    def _(step):
        for inner in range(PAIRS):
            level = 2 * (PAIRS * step + inner)
            operand = jnp.concatenate([damp_level(level), damp_level(level + 1)], 1)
            result = jnp.dot(mix[...], operand, preferred_element_type=F32)
            depth[level] = result[:, :cols]
            depth[level + 1] = result[:, cols:]

    stores = [pltpu.make_async_copy(out.at[pl.ds(1, fields - 1)], final.at[pl.ds(1, fields - 1)], finished.at[0])]
    stores[0].start()
    zero = jnp.zeros((half, cols), F32)
    log20 = math.log2(20.0)

    for part in range(rows // half):
        at = [band * rows + part * half for band in range(bands)]
        here = slice(part * half, (part + 1) * half)

        def forward(level, carry, last=False):
            carry = list(carry)
            emission = emit[level, here]
            for band in range(bands):
                g, h = carry[2 * band], carry[2 * band + 1]
                d = depth[level, at[band] : at[band] + half]
                if band < lwb:
                    source = d * emission
                else:
                    source = solar[band - lwb] * (1.0 - jnp.exp2(-LOG2E * d))
                q = (1.0 + d) + g
                w = source + h
                if last:
                    factor = zero
                    r = pl.reciprocal(q, approx=True)
                else:
                    coupling = jnp.exp2(log20 - (0.1 * LOG2E) * d)
                    r = pl.reciprocal(q + coupling, approx=True)
                    factor = coupling * r
                    carry[2 * band], carry[2 * band + 1] = factor * q, factor * w
                factors[level, at[band] : at[band] + half] = factor
                values[level, at[band] : at[band] + half] = w * r
            return tuple(carry)

        def forward_steps(step, carry):
            for inner in range(AHEAD):
                carry = forward(AHEAD * step + inner, carry)
            return carry

        carry = lax.fori_loop(0, levels // AHEAD - 1, forward_steps, (zero,) * (2 * bands))
        for level in range(levels - AHEAD, levels):
            carry = forward(level, carry, level == levels - 1)

        def backward(level, carry):
            carry = list(carry)
            emission = emit[level, here]
            lw, sw = zero, zero
            for band in range(bands):
                d = depth[level, at[band] : at[band] + half]
                x = (
                    values[level, at[band] : at[band] + half]
                    + factors[level, at[band] : at[band] + half] * carry[band]
                )
                carry[band] = x
                if band < lwb:
                    lw = lw + d * (x - emission)
                else:
                    sw = sw + d * x
            out[0, level, here] = out[0, level, here] + (time_step * lw + days[here] * sw)
            return tuple(carry)

        def backward_steps(step, carry):
            for inner in range(BACK):
                carry = backward(levels - 1 - BACK * step - inner, carry)
            return carry

        lax.fori_loop(0, levels // BACK, backward_steps, (zero,) * bands)
        stores.append(
            pltpu.make_async_copy(
                out.at[0, :, pl.ds(part * half, half)], final.at[0, :, pl.ds(part * half, half)], finished.at[part + 1]
            )
        )
        stores[-1].start()

    for copy in stores:
        copy.wait()


def shards(state, damping, k_longwave, k_shortwave, solar, daylight, cloud_top):
    fields, levels, rows, cols = state.shape
    bands = k_longwave.shape[0] + k_shortwave.shape[0]

    vmem = pl.BlockSpec(memory_space=pltpu.VMEM)
    smem = pl.BlockSpec(memory_space=pltpu.SMEM)
    edge_rows = jax.ShapeDtypeStruct((fields, levels, cols), F32)
    edge_cols = jax.ShapeDtypeStruct((fields, rows, cols), F32)
    mixing = jax.ShapeDtypeStruct((bands * rows, PARTS * rows), BF16)
    halos = pl.pallas_call(
        functools.partial(exchange, (lax.axis_size("gx"), lax.axis_size("gy"))),
        out_shape=[edge_rows, edge_rows, edge_cols, edge_cols, jax.ShapeDtypeStruct(state.shape, F32), mixing],
        in_specs=[smem, pl.BlockSpec(memory_space=pltpu.HBM), vmem, vmem],
        out_specs=[vmem] * 6,
        scratch_shapes=[
            pltpu.VMEM(state.shape, F32),
            pltpu.VMEM(edge_rows.shape, F32),
            pltpu.VMEM(edge_rows.shape, F32),
            pltpu.VMEM(edge_cols.shape, F32),
            pltpu.SemaphoreType.DMA((fields,)),
            pltpu.SemaphoreType.DMA((4,)),
            pltpu.SemaphoreType.DMA((4,)),
        ],
        compiler_params=pltpu.CompilerParams(
            collective_id=0, has_side_effects=True, vmem_limit_bytes=60 * 1024 * 1024
        ),
        name="exchange",
    )(damping, state, k_longwave.T, k_shortwave.T)
    return pl.pallas_call(
        kernel,
        out_shape=jax.ShapeDtypeStruct(state.shape, F32),
        in_specs=[smem, smem] + [vmem] * 8,
        out_specs=pl.BlockSpec(memory_space=pl.ANY),
        scratch_shapes=[
            pltpu.VMEM(state.shape, F32),
            pltpu.VMEM((fields, rows, cols), F32),
            pltpu.VMEM((levels, rows, cols), F32),
            pltpu.VMEM((levels, bands * rows, cols), F32),
            pltpu.VMEM((levels, bands * rows, cols), F32),
            pltpu.VMEM((levels, bands * rows, cols), F32),
            pltpu.SemaphoreType.DMA((1 + rows // 8,)),
        ],
        compiler_params=pltpu.CompilerParams(vmem_limit_bytes=48 * 1024 * 1024),
        cost_estimate=pl.CostEstimate(flops=100_000_000, bytes_accessed=4_000_000, transcendentals=5_000_000),
    )(damping, solar, *halos, daylight, cloud_top)


def solution(mesh):
    in_specs = (P(None, None, "gx", "gy"), P(), P(), P(), P(), P("gy", None), P("gy", None))
    out_specs = P(None, None, "gx", "gy")
    return jax.shard_map(shards, mesh=mesh, in_specs=in_specs, out_specs=out_specs, check_vma=False)
```

```python
import functools
import math

import jax
import numpy as np
import jax.numpy as jnp
from jax import lax
from jax.experimental import pallas as pl
from jax.experimental.pallas import tpu as pltpu
from jax.sharding import PartitionSpec as P

time_step = 0.1
F32 = jnp.float32
BF16 = jnp.bfloat16
LOG2E = math.log2(math.e)
PARTS = 14


PAIRS, AHEAD, BACK = 8, 8, 8


def split(value):
    high = value.astype(BF16)
    low = (value - high.astype(F32)).astype(BF16)
    return high, low


def build_mixing(mix, k_ref, first, cloud_depth, rows):
    bands = k_ref.shape[1]
    width = mix.shape[1]
    group = lax.broadcasted_iota(jnp.int32, (bands, width), 1) // rows
    same = lax.broadcasted_iota(jnp.int32, (bands, bands), 0) == lax.broadcasted_iota(
        jnp.int32, (bands, bands), 1
    )
    cloud_high = float(np.asarray(cloud_depth, dtype=BF16))
    spread = jnp.where(group == 12, cloud_high, jnp.where(group == 13, cloud_depth - cloud_high, 0.0))
    for field in range(4):
        weights = jnp.broadcast_to(k_ref[field : field + 1, :], (bands, bands))
        weights = jnp.sum(jnp.where(same, weights, 0.0), axis=1, keepdims=True)
        high, low = split(jnp.broadcast_to(weights, (bands, width)))
        high, low = high.astype(F32), low.astype(F32)
        spread = jnp.where((group == field) | (group == field + 8), high, spread)
        spread = jnp.where(group == field + 4, low, spread)
    lane = lax.broadcasted_iota(jnp.int32, (rows, width), 1)
    row = lax.broadcasted_iota(jnp.int32, (rows, width), 0)
    own = lane % rows == row
    for band in range(bands):
        block = jnp.broadcast_to(spread[band : band + 1], (rows, width))
        mix[(first + band) * rows : (first + band + 1) * rows] = jnp.where(own, block, 0.0).astype(BF16)


def exchange(
    shape, damping, source, k_lw, k_sw, north, south, west, east, partial, mix,
    state, first, final, packed, load, send, recv,
):
    n_gx, n_gy = shape
    fields, levels, rows, cols = source.shape
    loads = [pltpu.make_async_copy(source.at[field], state.at[field], load.at[field]) for field in range(fields)]
    for copy in loads:
        copy.start()
    gx, gy = lax.axis_index("gx"), lax.axis_index("gy")
    after, before = lax.rem(gx + 1, n_gx), lax.rem(gx + n_gx - 1, n_gx)
    right, left = lax.rem(gy + 1, n_gy), lax.rem(gy + n_gy - 1, n_gy)
    peers = ({"gx": after}, {"gx": before}, {"gy": right}, {"gy": left})

    barrier = pltpu.get_barrier_semaphore()
    for peer in peers:
        pl.semaphore_signal(barrier, inc=1, device_id=peer, device_id_type=pl.DeviceIdType.MESH)
    for field in range(fields):
        loads[field].wait()
        first[field] = state[field, :, 0, :]
        final[field] = state[field, :, rows - 1, :]
    pl.semaphore_wait(barrier, 4)

    moves = ((final, north), (first, south), (packed, west), (packed, east))
    copies = [
        pltpu.make_async_remote_copy(
            src_ref=origin,
            dst_ref=target,
            send_sem=send.at[index],
            recv_sem=recv.at[index],
            device_id=peers[index],
            device_id_type=pl.DeviceIdType.MESH,
        )
        for index, (origin, target) in enumerate(moves)
    ]
    copies[0].start()
    copies[1].start()
    pair = lax.broadcasted_iota(jnp.int32, (rows, cols), 1) // 2

    def pack(step, held):
        held = list(held)
        for inner in range(8):
            level = 8 * step + inner
            for field in range(fields):
                turned = pltpu.roll(state[field, level], 2 * level + 1, 1)
                held[field] = jnp.where(pair == level, turned, held[field])
        return tuple(held)

    held = lax.fori_loop(0, levels // 8, pack, (jnp.zeros((rows, cols), F32),) * fields)
    for field in range(fields):
        packed[field] = held[field]
    copies[2].start()
    copies[3].start()

    build_mixing(mix, k_lw, 0, 0.5, rows)
    build_mixing(mix, k_sw, k_lw.shape[1], 0.3, rows)
    lane = lax.broadcasted_iota(jnp.int32, (rows, cols), 1)
    row = lax.broadcasted_iota(jnp.int32, (rows, cols), 0)

    @pl.loop(0, levels // 4)
    def _(step):
        for inner in range(4):
            level = 4 * step + inner
            for field in range(fields):
                centre = state[field, level]
                up = jnp.where(row == 0, 0.0, pltpu.roll(centre, 1, 0))
                down = jnp.where(row == rows - 1, 0.0, pltpu.roll(centre, rows - 1, 0))
                before_lane = jnp.where(lane == 0, 0.0, pltpu.roll(centre, 1, 1))
                after_lane = jnp.where(lane == cols - 1, 0.0, pltpu.roll(centre, cols - 1, 1))
                laplace = (up + down) + (before_lane + after_lane) - 4.0 * centre
                partial[field, level] = centre + damping[field, level] * laplace

    for copy in copies:
        copy.wait()


def kernel(
    damping, solar, north, south, west, east, partial, mix, daylight, cloud_top, final,
    out, sides, emit, depth, factors, values, finished,
):
    fields, levels, rows, cols = partial.shape
    swb = solar.shape[0]
    bands = mix.shape[0] // rows
    lwb = bands - swb
    half = 8
    me = lax.axis_index("gx")

    lane = lax.broadcasted_iota(jnp.int32, (rows, cols), 1)
    row = lax.broadcasted_iota(jnp.int32, (rows, cols), 0)
    total = cloud_top.shape[1]
    wide_lane = lax.broadcasted_iota(jnp.int32, (rows, total), 1)
    wide_row = lax.broadcasted_iota(jnp.int32, (rows, total), 0)
    mine = wide_lane == me * rows + wide_row
    tops = jnp.sum(jnp.where(mine, cloud_top[...].astype(F32), 0.0), axis=1, keepdims=True)
    tops = jnp.broadcast_to(tops, (rows, cols)).astype(jnp.int32)
    days = jnp.sum(jnp.where(mine, daylight[...].astype(F32), 0.0), axis=1, keepdims=True)
    days = time_step * jnp.broadcast_to(days, (rows, cols))

    for field in range(fields):
        turned = pltpu.roll(east[field], cols - 2, 1)
        sides[field] = jnp.where(lane % 2 == 0, west[field], turned)

    border = (lane == 0) | (lane == cols - 1)

    def damp_level(level):
        cloudy = jnp.where(level >= tops, 1.0, 0.0).astype(F32)
        highs, lows = [], []
        for field in range(fields):
            beside = jnp.where(row == rows - 1, south[field, pl.ds(level, 1)], 0.0)
            beside = jnp.where(row == 0, north[field, pl.ds(level, 1)], beside)
            side = pltpu.roll(sides[field], lax.rem(cols - 2 * level, cols), 1)
            beside = beside + jnp.where(border, side, 0.0)
            damped = partial[field, level] + damping[field, level] * beside
            if field == 0:
                emit[level] = jnp.exp(0.3 * jnp.tanh(damped))
            if field == 1:
                out[field, level] = damped - (2.0 * time_step) * cloudy * damped
            else:
                out[field, level] = damped
            high, low = split(damped * damped)
            highs.append(high)
            lows.append(low)
        cloud = cloudy.astype(BF16)
        return jnp.concatenate(highs + highs + lows + [cloud, cloud], 0)

    @pl.loop(0, levels // (2 * PAIRS))
    def _(step):
        for inner in range(PAIRS):
            level = 2 * (PAIRS * step + inner)
            operand = jnp.concatenate([damp_level(level), damp_level(level + 1)], 1)
            result = jnp.dot(mix[...], operand, preferred_element_type=F32)
            depth[level] = result[:, :cols]
            depth[level + 1] = result[:, cols:]

    stores = [pltpu.make_async_copy(out.at[pl.ds(1, fields - 1)], final.at[pl.ds(1, fields - 1)], finished.at[0])]
    stores[0].start()
    zero = jnp.zeros((half, cols), F32)
    log20 = math.log2(20.0)

    for part in range(rows // half):
        at = [band * rows + part * half for band in range(bands)]
        here = slice(part * half, (part + 1) * half)

        def forward(level, carry, last=False):
            carry = list(carry)
            emission = emit[level, here]
            for band in range(bands):
                g, h = carry[2 * band], carry[2 * band + 1]
                d = depth[level, at[band] : at[band] + half]
                if band < lwb:
                    source = d * emission
                else:
                    source = solar[band - lwb] * (1.0 - jnp.exp2(-LOG2E * d))
                q = (1.0 + d) + g
                w = source + h
                if last:
                    factor = zero
                    r = pl.reciprocal(q, approx=True)
                else:
                    coupling = jnp.exp2(log20 - (0.1 * LOG2E) * d)
                    r = pl.reciprocal(q + coupling, approx=True)
                    factor = coupling * r
                    carry[2 * band], carry[2 * band + 1] = factor * q, factor * w
                factors[level, at[band] : at[band] + half] = factor
                values[level, at[band] : at[band] + half] = w * r
            return tuple(carry)

        def forward_steps(step, carry):
            for inner in range(AHEAD):
                carry = forward(AHEAD * step + inner, carry)
            return carry

        carry = lax.fori_loop(0, levels // AHEAD - 1, forward_steps, (zero,) * (2 * bands))
        for level in range(levels - AHEAD, levels):
            carry = forward(level, carry, level == levels - 1)

        def backward(level, carry):
            carry = list(carry)
            emission = emit[level, here]
            lw, sw = zero, zero
            for band in range(bands):
                d = depth[level, at[band] : at[band] + half]
                x = (
                    values[level, at[band] : at[band] + half]
                    + factors[level, at[band] : at[band] + half] * carry[band]
                )
                carry[band] = x
                if band < lwb:
                    lw = lw + d * (x - emission)
                else:
                    sw = sw + d * x
            out[0, level, here] = out[0, level, here] + (time_step * lw + days[here] * sw)
            return tuple(carry)

        def backward_steps(step, carry):
            for inner in range(BACK):
                carry = backward(levels - 1 - BACK * step - inner, carry)
            return carry

        lax.fori_loop(0, levels // BACK, backward_steps, (zero,) * bands)
        stores.append(
            pltpu.make_async_copy(
                out.at[0, :, pl.ds(part * half, half)], final.at[0, :, pl.ds(part * half, half)], finished.at[part + 1]
            )
        )
        stores[-1].start()

    for copy in stores:
        copy.wait()


def shards(state, damping, k_longwave, k_shortwave, solar, daylight, cloud_top):
    fields, levels, rows, cols = state.shape
    bands = k_longwave.shape[0] + k_shortwave.shape[0]

    vmem = pl.BlockSpec(memory_space=pltpu.VMEM)
    smem = pl.BlockSpec(memory_space=pltpu.SMEM)
    edge_rows = jax.ShapeDtypeStruct((fields, levels, cols), F32)
    edge_cols = jax.ShapeDtypeStruct((fields, rows, cols), F32)
    mixing = jax.ShapeDtypeStruct((bands * rows, PARTS * rows), BF16)
    halos = pl.pallas_call(
        functools.partial(exchange, (lax.axis_size("gx"), lax.axis_size("gy"))),
        out_shape=[edge_rows, edge_rows, edge_cols, edge_cols, jax.ShapeDtypeStruct(state.shape, F32), mixing],
        in_specs=[smem, pl.BlockSpec(memory_space=pltpu.HBM), vmem, vmem],
        out_specs=[vmem] * 6,
        scratch_shapes=[
            pltpu.VMEM(state.shape, F32),
            pltpu.VMEM(edge_rows.shape, F32),
            pltpu.VMEM(edge_rows.shape, F32),
            pltpu.VMEM(edge_cols.shape, F32),
            pltpu.SemaphoreType.DMA((fields,)),
            pltpu.SemaphoreType.DMA((4,)),
            pltpu.SemaphoreType.DMA((4,)),
        ],
        compiler_params=pltpu.CompilerParams(
            collective_id=0, has_side_effects=True, vmem_limit_bytes=51 * 1024 * 1024
        ),
        name="exchange",
    )(damping, state, k_longwave.T, k_shortwave.T)
    return pl.pallas_call(
        kernel,
        out_shape=jax.ShapeDtypeStruct(state.shape, F32),
        in_specs=[smem, smem] + [vmem] * 8,
        out_specs=pl.BlockSpec(memory_space=pl.ANY),
        scratch_shapes=[
            pltpu.VMEM(state.shape, F32),
            pltpu.VMEM((fields, rows, cols), F32),
            pltpu.VMEM((levels, rows, cols), F32),
            pltpu.VMEM((levels, bands * rows, cols), F32),
            pltpu.VMEM((levels, bands * rows, cols), F32),
            pltpu.VMEM((levels, bands * rows, cols), F32),
            pltpu.SemaphoreType.DMA((1 + rows // 8,)),
        ],
        compiler_params=pltpu.CompilerParams(vmem_limit_bytes=48 * 1024 * 1024),
        cost_estimate=pl.CostEstimate(flops=100_000_000, bytes_accessed=4_000_000, transcendentals=5_000_000),
    )(damping, solar, *halos, daylight, cloud_top)


def solution(mesh):
    in_specs = (P(None, None, "gx", "gy"), P(), P(), P(), P(), P("gy", None), P("gy", None))
    out_specs = P(None, None, "gx", "gy")
    return jax.shard_map(shards, mesh=mesh, in_specs=in_specs, out_specs=out_specs, check_vma=False)
```

```python
import functools
import math

import jax
import numpy as np
import jax.numpy as jnp
from jax import lax
from jax.experimental import pallas as pl
from jax.experimental.pallas import tpu as pltpu
from jax.sharding import PartitionSpec as P

time_step = 0.1
F32 = jnp.float32
BF16 = jnp.bfloat16
LOG2E = math.log2(math.e)
PARTS = 14


PAIRS, AHEAD, BACK = 16, 16, 16


def split(value):
    high = value.astype(BF16)
    low = (value - high.astype(F32)).astype(BF16)
    return high, low


def build_mixing(mix, k_ref, first, cloud_depth, rows):
    bands = k_ref.shape[1]
    width = mix.shape[1]
    group = lax.broadcasted_iota(jnp.int32, (bands, width), 1) // rows
    same = lax.broadcasted_iota(jnp.int32, (bands, bands), 0) == lax.broadcasted_iota(
        jnp.int32, (bands, bands), 1
    )
    cloud_high = float(np.asarray(cloud_depth, dtype=BF16))
    spread = jnp.where(group == 12, cloud_high, jnp.where(group == 13, cloud_depth - cloud_high, 0.0))
    for field in range(4):
        weights = jnp.broadcast_to(k_ref[field : field + 1, :], (bands, bands))
        weights = jnp.sum(jnp.where(same, weights, 0.0), axis=1, keepdims=True)
        high, low = split(jnp.broadcast_to(weights, (bands, width)))
        high, low = high.astype(F32), low.astype(F32)
        spread = jnp.where((group == field) | (group == field + 8), high, spread)
        spread = jnp.where(group == field + 4, low, spread)
    lane = lax.broadcasted_iota(jnp.int32, (rows, width), 1)
    row = lax.broadcasted_iota(jnp.int32, (rows, width), 0)
    own = lane % rows == row
    for band in range(bands):
        block = jnp.broadcast_to(spread[band : band + 1], (rows, width))
        mix[(first + band) * rows : (first + band + 1) * rows] = jnp.where(own, block, 0.0).astype(BF16)


def exchange(
    shape, damping, source, north, south, west, east, partial,
    state, first, final, packed, load, send, recv,
):
    n_gx, n_gy = shape
    fields, levels, rows, cols = source.shape
    loads = [pltpu.make_async_copy(source.at[field], state.at[field], load.at[field]) for field in range(fields)]
    for copy in loads:
        copy.start()
    gx, gy = lax.axis_index("gx"), lax.axis_index("gy")
    after, before = lax.rem(gx + 1, n_gx), lax.rem(gx + n_gx - 1, n_gx)
    right, left = lax.rem(gy + 1, n_gy), lax.rem(gy + n_gy - 1, n_gy)
    peers = ({"gx": after}, {"gx": before}, {"gy": right}, {"gy": left})

    barrier = pltpu.get_barrier_semaphore()
    for peer in peers:
        pl.semaphore_signal(barrier, inc=1, device_id=peer, device_id_type=pl.DeviceIdType.MESH)
    for field in range(fields):
        loads[field].wait()
        first[field] = state[field, :, 0, :]
        final[field] = state[field, :, rows - 1, :]
    pl.semaphore_wait(barrier, 4)

    moves = ((final, north), (first, south), (packed, west), (packed, east))
    copies = [
        pltpu.make_async_remote_copy(
            src_ref=origin,
            dst_ref=target,
            send_sem=send.at[index],
            recv_sem=recv.at[index],
            device_id=peers[index],
            device_id_type=pl.DeviceIdType.MESH,
        )
        for index, (origin, target) in enumerate(moves)
    ]
    copies[0].start()
    copies[1].start()
    pair = lax.broadcasted_iota(jnp.int32, (rows, cols), 1) // 2

    def pack(step, held):
        held = list(held)
        for inner in range(8):
            level = 8 * step + inner
            for field in range(fields):
                turned = pltpu.roll(state[field, level], 2 * level + 1, 1)
                held[field] = jnp.where(pair == level, turned, held[field])
        return tuple(held)

    held = lax.fori_loop(0, levels // 8, pack, (jnp.zeros((rows, cols), F32),) * fields)
    for field in range(fields):
        packed[field] = held[field]
    copies[2].start()
    copies[3].start()

    lane = lax.broadcasted_iota(jnp.int32, (rows, cols), 1)
    row = lax.broadcasted_iota(jnp.int32, (rows, cols), 0)

    @pl.loop(0, levels // 4)
    def _(step):
        for inner in range(4):
            level = 4 * step + inner
            for field in range(fields):
                centre = state[field, level]
                up = jnp.where(row == 0, 0.0, pltpu.roll(centre, 1, 0))
                down = jnp.where(row == rows - 1, 0.0, pltpu.roll(centre, rows - 1, 0))
                before_lane = jnp.where(lane == 0, 0.0, pltpu.roll(centre, 1, 1))
                after_lane = jnp.where(lane == cols - 1, 0.0, pltpu.roll(centre, cols - 1, 1))
                laplace = (up + down) + (before_lane + after_lane) - 4.0 * centre
                partial[field, level] = centre + damping[field, level] * laplace

    for copy in copies:
        copy.wait()


def kernel(
    damping, solar, north, south, west, east, partial, k_lw, k_sw, daylight, cloud_top, final,
    out, mix, sides, emit, depth, factors, values, finished,
):
    fields, levels, rows, cols = partial.shape
    lwb, swb = k_lw.shape[1], k_sw.shape[1]
    bands = lwb + swb
    half = 8
    me = lax.axis_index("gx")

    build_mixing(mix, k_lw, 0, 0.5, rows)
    build_mixing(mix, k_sw, lwb, 0.3, rows)
    lane = lax.broadcasted_iota(jnp.int32, (rows, cols), 1)
    row = lax.broadcasted_iota(jnp.int32, (rows, cols), 0)
    total = cloud_top.shape[1]
    wide_lane = lax.broadcasted_iota(jnp.int32, (rows, total), 1)
    wide_row = lax.broadcasted_iota(jnp.int32, (rows, total), 0)
    mine = wide_lane == me * rows + wide_row
    tops = jnp.sum(jnp.where(mine, cloud_top[...].astype(F32), 0.0), axis=1, keepdims=True)
    tops = jnp.broadcast_to(tops, (rows, cols)).astype(jnp.int32)
    days = jnp.sum(jnp.where(mine, daylight[...].astype(F32), 0.0), axis=1, keepdims=True)
    days = time_step * jnp.broadcast_to(days, (rows, cols))

    for field in range(fields):
        turned = pltpu.roll(east[field], cols - 2, 1)
        sides[field] = jnp.where(lane % 2 == 0, west[field], turned)

    border = (lane == 0) | (lane == cols - 1)

    def damp_level(level):
        cloudy = jnp.where(level >= tops, 1.0, 0.0).astype(F32)
        highs, lows = [], []
        for field in range(fields):
            beside = jnp.where(row == rows - 1, south[field, pl.ds(level, 1)], 0.0)
            beside = jnp.where(row == 0, north[field, pl.ds(level, 1)], beside)
            side = pltpu.roll(sides[field], lax.rem(cols - 2 * level, cols), 1)
            beside = beside + jnp.where(border, side, 0.0)
            damped = partial[field, level] + damping[field, level] * beside
            if field == 0:
                emit[level] = jnp.exp(0.3 * jnp.tanh(damped))
            if field == 1:
                out[field, level] = damped - (2.0 * time_step) * cloudy * damped
            else:
                out[field, level] = damped
            high, low = split(damped * damped)
            highs.append(high)
            lows.append(low)
        cloud = cloudy.astype(BF16)
        return jnp.concatenate(highs + highs + lows + [cloud, cloud], 0)

    @pl.loop(0, levels // (2 * PAIRS))
    def _(step):
        for inner in range(PAIRS):
            level = 2 * (PAIRS * step + inner)
            operand = jnp.concatenate([damp_level(level), damp_level(level + 1)], 1)
            result = jnp.dot(mix[...], operand, preferred_element_type=F32)
            depth[level] = result[:, :cols]
            depth[level + 1] = result[:, cols:]

    stores = [pltpu.make_async_copy(out.at[pl.ds(1, fields - 1)], final.at[pl.ds(1, fields - 1)], finished.at[0])]
    stores[0].start()
    zero = jnp.zeros((half, cols), F32)
    log20 = math.log2(20.0)

    for part in range(rows // half):
        at = [band * rows + part * half for band in range(bands)]
        here = slice(part * half, (part + 1) * half)

        def forward(level, carry, last=False):
            carry = list(carry)
            emission = emit[level, here]
            for band in range(bands):
                g, h = carry[2 * band], carry[2 * band + 1]
                d = depth[level, at[band] : at[band] + half]
                if band < lwb:
                    source = d * emission
                else:
                    source = solar[band - lwb] * (1.0 - jnp.exp2(-LOG2E * d))
                q = (1.0 + d) + g
                w = source + h
                if last:
                    factor = zero
                    r = pl.reciprocal(q, approx=True)
                else:
                    coupling = jnp.exp2(log20 - (0.1 * LOG2E) * d)
                    r = pl.reciprocal(q + coupling, approx=True)
                    factor = coupling * r
                    carry[2 * band], carry[2 * band + 1] = factor * q, factor * w
                factors[level, at[band] : at[band] + half] = factor
                values[level, at[band] : at[band] + half] = w * r
            return tuple(carry)

        def forward_steps(step, carry):
            for inner in range(AHEAD):
                carry = forward(AHEAD * step + inner, carry)
            return carry

        carry = lax.fori_loop(0, levels // AHEAD - 1, forward_steps, (zero,) * (2 * bands))
        for level in range(levels - AHEAD, levels):
            carry = forward(level, carry, level == levels - 1)

        def backward(level, carry):
            carry = list(carry)
            emission = emit[level, here]
            lw, sw = zero, zero
            for band in range(bands):
                d = depth[level, at[band] : at[band] + half]
                x = (
                    values[level, at[band] : at[band] + half]
                    + factors[level, at[band] : at[band] + half] * carry[band]
                )
                carry[band] = x
                if band < lwb:
                    lw = lw + d * (x - emission)
                else:
                    sw = sw + d * x
            out[0, level, here] = out[0, level, here] + (time_step * lw + days[here] * sw)
            return tuple(carry)

        def backward_steps(step, carry):
            for inner in range(BACK):
                carry = backward(levels - 1 - BACK * step - inner, carry)
            return carry

        lax.fori_loop(0, levels // BACK, backward_steps, (zero,) * bands)
        stores.append(
            pltpu.make_async_copy(
                out.at[0, :, pl.ds(part * half, half)], final.at[0, :, pl.ds(part * half, half)], finished.at[part + 1]
            )
        )
        stores[-1].start()

    for copy in stores:
        copy.wait()


def shards(state, damping, k_longwave, k_shortwave, solar, daylight, cloud_top):
    fields, levels, rows, cols = state.shape
    bands = k_longwave.shape[0] + k_shortwave.shape[0]

    vmem = pl.BlockSpec(memory_space=pltpu.VMEM)
    smem = pl.BlockSpec(memory_space=pltpu.SMEM)
    edge_rows = jax.ShapeDtypeStruct((fields, levels, cols), F32)
    edge_cols = jax.ShapeDtypeStruct((fields, rows, cols), F32)
    halos = pl.pallas_call(
        functools.partial(exchange, (lax.axis_size("gx"), lax.axis_size("gy"))),
        out_shape=[edge_rows, edge_rows, edge_cols, edge_cols, jax.ShapeDtypeStruct(state.shape, F32)],
        in_specs=[smem, pl.BlockSpec(memory_space=pltpu.HBM)],
        out_specs=[vmem] * 5,
        scratch_shapes=[
            pltpu.VMEM(state.shape, F32),
            pltpu.VMEM(edge_rows.shape, F32),
            pltpu.VMEM(edge_rows.shape, F32),
            pltpu.VMEM(edge_cols.shape, F32),
            pltpu.SemaphoreType.DMA((fields,)),
            pltpu.SemaphoreType.DMA((4,)),
            pltpu.SemaphoreType.DMA((4,)),
        ],
        compiler_params=pltpu.CompilerParams(
            collective_id=0, has_side_effects=True, vmem_limit_bytes=51 * 1024 * 1024
        ),
        name="exchange",
    )(damping, state)
    return pl.pallas_call(
        kernel,
        out_shape=jax.ShapeDtypeStruct(state.shape, F32),
        in_specs=[smem, smem] + [vmem] * 9,
        out_specs=pl.BlockSpec(memory_space=pl.ANY),
        scratch_shapes=[
            pltpu.VMEM(state.shape, F32),
            pltpu.VMEM((bands * rows, PARTS * rows), BF16),
            pltpu.VMEM((fields, rows, cols), F32),
            pltpu.VMEM((levels, rows, cols), F32),
            pltpu.VMEM((levels, bands * rows, cols), F32),
            pltpu.VMEM((levels, bands * rows, cols), F32),
            pltpu.VMEM((levels, bands * rows, cols), F32),
            pltpu.SemaphoreType.DMA((1 + rows // 8,)),
        ],
        compiler_params=pltpu.CompilerParams(vmem_limit_bytes=48 * 1024 * 1024),
        cost_estimate=pl.CostEstimate(flops=100_000_000, bytes_accessed=4_000_000, transcendentals=5_000_000),
    )(damping, solar, *halos, k_longwave.T, k_shortwave.T, daylight, cloud_top)


def solution(mesh):
    in_specs = (P(None, None, "gx", "gy"), P(), P(), P(), P(), P("gy", None), P("gy", None))
    out_specs = P(None, None, "gx", "gy")
    return jax.shard_map(shards, mesh=mesh, in_specs=in_specs, out_specs=out_specs, check_vma=False)
```
